32 devices in a mesh: groups: 2 (over y), space: 4 (over z), comp: 2 (over x), sub: 2 (over core).
Axes of the slice: x: 2, y: 2, z: 4, core: 2. Of those that a mesh axis runs over, the one named last changes fastest.
Arguments:
- spectrum: float32 [32, 512, 864], P(('groups', 'sub'), ('space', 'comp')), parts along dimension 0, may hold values from 0.05 to 1
- wind_speed: float32 [32, 512], P(('groups', 'sub'), ('space', 'comp')), parts along dimension 0, may hold values from 2 to 10
- wind_dir: float32 [32, 512], P(('groups', 'sub'), ('space', 'comp')), parts along dimension 0, may hold values from -3.140625 to 3.140625
- ocean_mask: int32 [16, 512], P('sub', 'space'), may hold values 0 or 1
- turning: float32 [16, 512], P('sub', 'space'), may hold values from -0.8 to 0.8
- u_current: float32 [16], P('sub'), may hold values from -0.35 to 0.35
- group_courant: float32 [24], replicated, may hold values from 0.2 to 0.55
- growth_rate: float32 [24], replicated, may hold values from 0.02 to 0.08
- dissipation: float32 [24], replicated, may hold values from 0.2 to 0.6
- comp_owner: int32 [24], replicated, may hold values from 0 to 23, each once
Outputs:
- propagated: float32 [24, 36, 32, 512], P('comp', None, ('groups', 'sub'), 'space'), parts along dimension 2
The draws below stay inside these ranges and needn't reach their ends.
There are 2 independent parts, one for each index of `groups`. The reference program is written for one: setup_inputs(seed, part) draws one part's arguments, and reference() takes and returns one part's arrays. A program takes and returns all parts, laid end to end along the dimension named above; an argument that names none is the same for every part. Nothing has to cross between parts.
Inputs may be any that keep to these rules, and one draw needn't show every extreme that they name: `comp_owner`: each of the 24 frequencies appears once.
All inputs are finite; a program needn't handle non-finite values. No bound on the sum of `ocean_mask` on one device may be relied on, other than what follows from the above.
Results may differ from the reference program's by a relative error of at most 0.0003.
Values sent between devices are 32-bit elements; how exact they have to be, the bound alone decides.
A program may use at most 128 MiB of HBM per device.

```python
import math
import jax
import jax.numpy as jnp
from jax import lax

NDIR = 36
NFREQ = 24
NSUB = 4
NCOMP = 864
NLAT = 16
NLON = 512


def plant(result, key, low, largest):
    dims = result.shape
    place = [jax.random.randint(jax.random.fold_in(key, axis), (), 0, dims[axis]) for axis in range(len(dims))]
    result = result.at[tuple(place)].set(low)
    longest = dims.index(max(dims))
    place[longest] = (place[longest] + 1) % dims[longest]
    return result.at[tuple(place)].set(largest)


def level_of(own_key, dims, cuts, low, high):
    def one(dim, shards_of):
        steps = jax.random.uniform(jax.random.fold_in(jax.random.fold_in(own_key, 6), dim), (shards_of,), jnp.float32, low / len(cuts), high / len(cuts))
        return jnp.repeat(jnp.exp(steps), dims[dim] // shards_of).reshape((-1,) + (1,) * (len(dims) - dim - 1))

    loudness = one(*cuts[0])
    for cut in cuts[1:]:
        loudness = loudness * one(*cut)
    return loudness


def setup_inputs(seed: int = 0, part: int = 0) -> dict:
    splits = jax.random.split(jax.random.key(seed), 11)
    part_splits = jax.random.split(jax.random.fold_in(splits[10], part), 11)
    spectrum = jnp.clip(jnp.exp(math.log(1.0) - 2.9957323 * jax.random.uniform(part_splits[0], (NLAT, NLON, NCOMP), jnp.float32) ** level_of(part_splits[0], (NLAT, NLON, NCOMP), ((0, 2), (1, 8)), -0.2, 0.2)), 0.05, 1.0)
    wind_speed = jnp.clip(jnp.exp(math.log(10.0) - 1.609438 * jax.random.uniform(part_splits[1], (NLAT, NLON), jnp.float32) ** level_of(part_splits[1], (NLAT, NLON), ((0, 2), (1, 8)), -0.2, 0.2)), 2.0, 10.0)
    wind_dir = jnp.clip(jax.random.uniform(part_splits[2], (NLAT, NLON), jnp.float32, -3.140625, 3.140625), -3.140625, 3.140625)
    ocean_mask = plant((jax.random.randint(splits[3], (NLAT, NLON), 0, 4) < 3).astype(jnp.int32), jax.random.fold_in(splits[3], 1), 0, 1)
    turning = jnp.clip(jax.random.uniform(splits[4], (NLAT, NLON), jnp.float32, -0.8, 0.8) * level_of(splits[4], (NLAT, NLON), ((0, 2), (1, 4)), -0.4, 0.0), -0.8, 0.8)
    u_current = jnp.clip(jax.random.uniform(splits[5], (NLAT,), jnp.float32, -0.35, 0.35) * level_of(splits[5], (NLAT,), ((0, 2),), -0.4, 0.0), -0.35, 0.35)
    group_courant = jnp.clip(jnp.exp(jax.random.uniform(splits[6], (NFREQ,), jnp.float32, math.log(0.2), math.log(0.55))), 0.2, 0.55)
    growth_rate = jnp.clip(jnp.exp(jax.random.uniform(splits[7], (NFREQ,), jnp.float32, math.log(0.02), math.log(0.08))), 0.02, 0.08)
    dissipation = jnp.clip(jnp.exp(jax.random.uniform(splits[8], (NFREQ,), jnp.float32, math.log(0.2), math.log(0.6))), 0.2, 0.6)
    comp_owner = jax.random.permutation(splits[9], NFREQ).astype(jnp.int32)
    return {"spectrum": spectrum, "wind_speed": wind_speed, "wind_dir": wind_dir, "ocean_mask": ocean_mask, "turning": turning, "u_current": u_current, "group_courant": group_courant, "growth_rate": growth_rate, "dissipation": dissipation, "comp_owner": comp_owner}


def quickest(padded, courant, axis):
    count = padded.shape[axis] - 4
    left_far = lax.slice_in_dim(padded, 0, count + 1, axis=axis)
    left = lax.slice_in_dim(padded, 1, count + 2, axis=axis)
    right = lax.slice_in_dim(padded, 2, count + 3, axis=axis)
    right_far = lax.slice_in_dim(padded, 3, count + 4, axis=axis)
    curve = jnp.where(courant > 0, right - 2.0 * left + left_far, left - 2.0 * right + right_far)
    face = 0.5 * (left + right) - 0.5 * courant * (right - left) - (1.0 - courant * courant) / 6.0 * curve
    flux = courant * face
    center = lax.slice_in_dim(padded, 2, count + 2, axis=axis)
    return center - (lax.slice_in_dim(flux, 1, count + 1, axis=axis) - lax.slice_in_dim(flux, 0, count, axis=axis))


def source_terms(energy, wind_speed, wind_dir, growth_rate, dissipation):
    angles = 2.0 * math.pi * jnp.arange(NDIR, dtype=jnp.float32) / NDIR
    level = jnp.mean(energy, axis=(2, 3), keepdims=True)
    align = jnp.maximum(jnp.cos(angles[None, None, None, :] - wind_dir[:, :, None, None]), 0.0)
    growth = growth_rate[None, None, :, None] * wind_speed[:, :, None, None] * align
    loss = dissipation[None, None, :, None] * level / (level + 0.25)
    return energy * jnp.exp(growth - loss)


def reference(spectrum, wind_speed, wind_dir, ocean_mask, turning, u_current, group_courant, growth_rate, dissipation, comp_owner):
    energy = spectrum.reshape(NLAT, NLON, NFREQ, NDIR)
    source = source_terms(energy, wind_speed, wind_dir, growth_rate, dissipation)
    ordered = jnp.take(source, comp_owner, axis=2)
    maskf = ocean_mask.astype(jnp.float32)
    field = jnp.transpose(ordered, (2, 3, 0, 1)) * maskf
    angles = 2.0 * math.pi * jnp.arange(NDIR, dtype=jnp.float32) / NDIR
    speed = jnp.take(group_courant, comp_owner)
    along_x = speed[:, None, None, None] * jnp.cos(angles)[None, :, None, None] + u_current[None, None, :, None]
    along_y = speed[:, None, None, None] * jnp.sin(angles)[None, :, None, None]
    for step in range(NSUB):
        padded = jnp.concatenate([field[..., -2:], field, field[..., :2]], axis=3)
        field = quickest(padded, along_x, 3) * maskf
    for step in range(NSUB):
        padded = jnp.pad(field, ((0, 0), (0, 0), (2, 2), (0, 0)))
        field = quickest(padded, along_y, 2) * maskf
    for step in range(NSUB):
        padded = jnp.concatenate([field[:, -2:], field, field[:, :2]], axis=1)
        field = quickest(padded, turning[None, None], 1)
    return field
```

```python
import functools
import math

import jax
import jax.numpy as jnp
import numpy as np
from jax import lax
from jax.experimental import pallas as pl
from jax.experimental.pallas import tpu as pltpu
from jax.sharding import PartitionSpec as P

NSUB = 4
HALO = 2 * NSUB
PER_PACK = 12
ROWS = 8
LANES = 128


def weights(courant):
    s = jnp.abs(courant)
    q = (1.0 - s * s) / 6.0
    sq = s * q
    up2 = -sq
    up1 = s * (0.5 + 0.5 * s) + 3.0 * sq
    mid = 1.0 - s * s - 3.0 * sq
    down = sq - s * (0.5 - 0.5 * s)
    return up2, up1, mid, down


def kernel(
    sizes,
    xt,
    wind_speed,
    wind_dir,
    mask,
    turning,
    current,
    speed,
    growth,
    loss,
    owner,
    cosines,
    sines,
    out,
    tables,
    level_part,
    sendbuf,
    recv,
    main,
    small,
    small_sib,
    small_left,
    small_right,
    mask_all,
    turn_all,
    halo_out,
    halo_in,
    spin,
    res,
    send_sem,
    recv_sem,
    small_send,
    small_recv,
    halo_send,
    halo_recv,
    out_send,
    out_recv,
    own_sem,
):
    ncomp, nspace, ndirs, nfreqs, per_core = sizes
    strip = LANES // ncomp
    nd = ndirs // ncomp
    half = ndirs // 2
    packs = ndirs // PER_PACK
    me_c = lax.axis_index("comp")
    me_s = lax.axis_index("sub")
    me_z = lax.axis_index("space")
    other = 1 - me_s
    right = lax.rem(me_z + 1, nspace)
    left = lax.rem(me_z + nspace - 1, nspace)
    MESH = pl.DeviceIdType.MESH
    lane = lax.broadcasted_iota(jnp.int32, (ROWS, LANES), 1)
    row = lax.broadcasted_iota(jnp.int32, (ROWS, LANES), 0)

    def peer(co, so):
        return {"comp": lax.rem(me_c + co, ncomp), "sub": lax.rem(me_s + so, 2)}

    peers = [(co, so) for co in range(ncomp) for so in range(2) if co or so]
    near = [{"space": z, "sub": s} for z in (left, right) for s in (me_s, other)]
    barrier = pltpu.get_barrier_semaphore()
    for co, so in peers:
        pl.semaphore_signal(barrier, inc=1, device_id=peer(co, so), device_id_type=MESH)
    for to in near:
        pl.semaphore_signal(barrier, inc=1, device_id=to, device_id_type=MESH)

    level_part[...] = jnp.zeros_like(level_part)

    def add_level(f, carry):
        for part in range(4):
            block = xt[pl.ds(f * ndirs + part * (ndirs // 4), ndirs // 4)]
            level_part[part] += jnp.sum(block, axis=0)
        return carry

    lax.fori_loop(0, nfreqs, add_level, 0)
    level = (level_part[0] + level_part[1] + level_part[2] + level_part[3]) / (nfreqs * ndirs)
    level = level / (level + 0.25)

    def tiled(a):
        return jnp.concatenate([a] * ncomp, axis=1)

    level = tiled(level)
    wind = tiled(wind_speed[...])
    toward = tiled(wind_dir[...])
    group = (lane // strip) * nd
    for dd in range(nd):
        angle = 2.0 * math.pi * (group + dd).astype(jnp.float32) / ndirs
        tables[dd] = wind * jnp.maximum(jnp.cos(angle - toward), 0.0)

    small[0] = mask[...]
    small[1] = turning[...]
    small[2] = current[...]
    pl.semaphore_wait(barrier, len(peers) + len(near))

    def fill(dst, at, co, so, kk):
        dest = peer(co, so)
        k = (dest["comp"] * 2 + dest["sub"]) * per_core + kk
        f = owner[k]
        g_rate = growth[f]
        d_rate = loss[f]
        for dd in range(nd):
            parts = [xt[f * ndirs + g * nd + dd] for g in range(ncomp)]
            tile = jnp.concatenate(parts, axis=1)
            dst[at, kk, dd] = tile * jnp.exp(g_rate * tables[dd] - d_rate * level)

    def block_copy(co, so, kk):
        r = co * 2 + so
        return pltpu.make_async_remote_copy(
            src_ref=sendbuf.at[r, kk],
            dst_ref=recv.at[r, kk],
            send_sem=send_sem.at[r, kk],
            recv_sem=recv_sem.at[r, kk],
            device_id=peer(co, so),
            device_id_type=MESH,
        )

    def send_far(kk, carry):
        for co, so in peers:
            if co:
                fill(sendbuf, co * 2 + so, co, so, kk)
                block_copy(co, so, kk).start()
        return carry

    lax.fori_loop(0, per_core, send_far, 0)

    def small_copies():
        sib = pltpu.make_async_remote_copy(
            src_ref=small, dst_ref=small_sib, send_sem=small_send.at[0], recv_sem=small_recv.at[0],
            device_id={"sub": other}, device_id_type=MESH)
        copies = [sib]
        for n, (z, land) in enumerate(((right, small_left), (left, small_right))):
            for so in range(2):
                i = 1 + 2 * n + so
                copies.append(pltpu.make_async_remote_copy(
                    src_ref=small.at[0], dst_ref=land.at[so], send_sem=small_send.at[i],
                    recv_sem=small_recv.at[i],
                    device_id={"space": z, "sub": lax.rem(me_s + so, 2)}, device_id_type=MESH))
        return copies

    for copy in small_copies():
        copy.start()

    def send_near(kk, carry):
        fill(sendbuf, 1, 0, 1, kk)
        block_copy(0, 1, kk).start()
        fill(recv, 0, 0, 0, kk)
        return carry

    lax.fori_loop(0, per_core, send_near, 0)

    for copy in small_copies():
        copy.wait()

    first = me_s == 0

    def both(own, sib):
        return jnp.where(first, own, sib), jnp.where(first, sib, own)

    def windows(lo, hi, lo_left, hi_left, lo_right, hi_right):
        acc = jnp.zeros((ROWS, LANES), jnp.float32)
        for base, own, l_halo, r_halo in ((0, lo, lo_left, lo_right), (64, hi, hi_left, hi_right)):
            for tile, start, count, at in (
                (own, LANES - 16, 16, 0),
                (r_halo, 0, HALO, 16),
                (l_halo, LANES - HALO, HALO, 24),
                (own, 0, 16, 32),
            ):
                moved = pltpu.roll(tile, (base + at - start) % LANES, 1)
                here = (lane >= base + at) & (lane < base + at + count)
                acc = jnp.where(here, moved, acc)
        return acc

    lo, hi = both(small[0], small_sib[0])
    lo_left, hi_left = both(small_left[0], small_left[1])
    lo_right, hi_right = both(small_right[0], small_right[1])
    mask_all[0] = lo
    mask_all[1] = hi
    mask_all[2] = windows(lo, hi, lo_left, hi_left, lo_right, hi_right)
    lo, hi = both(small[1], small_sib[1])
    for h, c in ((0, lo), (1, hi)):
        for i, w in enumerate(weights(c)):
            turn_all[h, i] = w
        turn_all[h, 4] = c
    lo, hi = both(small[2], small_sib[2])
    mask_all[3] = lo
    mask_all[4] = hi
    mask_all[5] = jnp.where(lane < 64, lo, hi)

    def halo_copy(side, kk):
        to = left if side == 0 else right
        return pltpu.make_async_remote_copy(
            src_ref=halo_out.at[side, kk],
            dst_ref=halo_in.at[side, kk],
            send_sem=halo_send.at[side, kk],
            recv_sem=halo_recv.at[side, kk],
            device_id={"space": to},
            device_id_type=MESH,
        )

    def assemble(kk):
        for co, so in peers:
            block_copy(co, so, kk).wait_recv()
        for h in range(2):
            so = lax.rem(h + me_s, 2)
            sea = mask_all[h]
            for dd in range(nd):
                got = [recv[lax.rem(me_c + ncomp - c, ncomp) * 2 + so, kk, dd] for c in range(ncomp)]
                for g in range(ncomp):
                    tile = got[0] if g == 0 else pltpu.roll(got[0], (LANES - g * strip) % LANES, 1)
                    for c in range(1, ncomp):
                        part = got[c]
                        if c != g:
                            part = pltpu.roll(part, ((c - g) * strip) % LANES, 1)
                        tile = jnp.where(lane < c * strip, tile, part)
                    main[kk, h, g * nd + dd] = tile * sea
            for q in range(packs):
                lows = jnp.zeros((ROWS, LANES), jnp.float32)
                highs = lows
                for j in range(PER_PACK):
                    tile = main[kk, h, q * PER_PACK + j]
                    at = j * HALO
                    here = (lane >= at) & (lane < at + HALO)
                    low = tile if at == 0 else pltpu.roll(tile, at, 1)
                    lows = jnp.where(here, low, lows)
                    highs = jnp.where(here, pltpu.roll(tile, at + HALO, 1), highs)
                halo_out[0, kk, h * packs + q] = lows
                halo_out[1, kk, h * packs + q] = highs
        halo_copy(0, kk).start()
        halo_copy(1, kk).start()

    def along_lon(f, w, up, sea):
        up2, before, mid, after = w
        for _ in range(NSUB):
            far = jnp.where(up, pltpu.roll(f, 2, 1), pltpu.roll(f, LANES - 2, 1))
            near_sum = before * pltpu.roll(f, 1, 1) + after * pltpu.roll(f, LANES - 1, 1)
            f = (mid * f + up2 * far + near_sum) * sea
        return f

    def along_lat(lo, hi, c, forward, sea_lo, sea_hi):
        up2, up1, mid, down = weights(c)
        for _ in range(NSUB):
            if forward:
                a, b = lo, hi

                def shift(n):
                    ra, rb = pltpu.roll(a, n, 0), pltpu.roll(b, n, 0)
                    return jnp.where(row < n, 0.0, ra), jnp.where(row < n, ra, rb)

                rb1, ra1 = pltpu.roll(hi, ROWS - 1, 0), pltpu.roll(lo, ROWS - 1, 0)
                lo_dn = jnp.where(row < ROWS - 1, ra1, rb1)
                hi_dn = jnp.where(row < ROWS - 1, rb1, 0.0)
            else:
                a, b = lo, hi

                def shift(n):
                    ra, rb = pltpu.roll(a, ROWS - n, 0), pltpu.roll(b, ROWS - n, 0)
                    return jnp.where(row < ROWS - n, ra, rb), jnp.where(row < ROWS - n, rb, 0.0)

                ra1, rb1 = pltpu.roll(lo, 1, 0), pltpu.roll(hi, 1, 0)
                lo_dn = jnp.where(row < 1, 0.0, ra1)
                hi_dn = jnp.where(row < 1, ra1, rb1)
            lo1, hi1 = shift(1)
            lo2, hi2 = shift(2)
            lo = (mid * lo + up1 * lo1 + (up2 * lo2 + down * lo_dn)) * sea_lo
            hi = (mid * hi + up1 * hi1 + (up2 * hi2 + down * hi_dn)) * sea_hi
        return lo, hi

    def propagate(kk):
        halo_copy(0, kk).wait_recv()
        halo_copy(1, kk).wait_recv()
        k = (me_c * 2 + me_s) * per_core + kk
        pace = speed[owner[k]]

        def one(q, j, d, forward):
            lo, hi = main[kk, 0, d], main[kk, 1, d]
            edge = jnp.zeros((ROWS, LANES), jnp.float32)
            for h, tile in ((0, lo), (1, hi)):
                base = 64 * h
                before = halo_in[1, kk, h * packs + q]
                after = halo_in[0, kk, h * packs + q]
                for source, start, count, at in (
                    (tile, LANES - 16, 16, 0),
                    (after, j * HALO, HALO, 16),
                    (before, j * HALO, HALO, 24),
                    (tile, 0, 16, 32),
                ):
                    amount = (base + at - start) % LANES
                    moved = source if amount == 0 else pltpu.roll(source, amount, 1)
                    here = (lane >= base + at) & (lane < base + at + count)
                    edge = jnp.where(here, moved, edge)
            c0 = pace * cosines[d]
            done = []
            for i, tile in enumerate((lo, hi, edge)):
                c = c0 + mask_all[3 + i]
                up2, up1, mid, down = weights(c)
                up = c > 0
                w = (up2, jnp.where(up, up1, down), mid, jnp.where(up, down, up1))
                done.append(along_lon(tile, w, up, mask_all[i]))
            lo, hi, edge = done
            fixed = []
            for h, tile in ((0, lo), (1, hi)):
                base = 64 * h
                tile = jnp.where(lane < HALO, pltpu.roll(edge, (LANES - base - 32) % LANES, 1), tile)
                tile = jnp.where(
                    lane >= LANES - HALO, pltpu.roll(edge, (LANES - 16 - base) % LANES, 1), tile)
                fixed.append(tile)
            lo, hi = along_lat(fixed[0], fixed[1], pace * sines[d], forward, mask_all[0], mask_all[1])
            spin[0, 0, d] = lo
            spin[0, 1, d] = hi

        for d in range(ndirs):
            one(d // PER_PACK, d % PER_PACK, d, d < half)

        def turn(h, carry):
            up2, up1, mid, down = (turn_all[h, i] for i in range(4))
            up = turn_all[h, 4] > 0
            before, after = jnp.where(up, up1, down), jnp.where(up, down, up1)
            for step in range(NSUB):
                for d in range(ndirs):
                    f = [spin[step % 2, h, (d + n) % ndirs] for n in (-2, -1, 0, 1, 2)]
                    new = (mid * f[2] + up2 * jnp.where(up, f[0], f[4])) + (before * f[1] + after * f[3])
                    if step == NSUB - 1:
                        res[kk, h, d] = new
                    else:
                        spin[(step + 1) % 2, h, d] = new
            return carry

        lax.fori_loop(0, 2, turn, 0)
        for copy in out_copies(kk):
            copy.start()

    def out_copies(kk):
        slot = me_s * per_core + kk
        own = pltpu.make_async_copy(res.at[kk, me_s], out.at[slot], own_sem.at[kk])
        far = pltpu.make_async_remote_copy(
            src_ref=res.at[kk, other], dst_ref=out.at[slot], send_sem=out_send.at[kk],
            recv_sem=out_recv.at[kk], device_id={"sub": other}, device_id_type=MESH)
        return own, far

    def run(kk, carry):
        @pl.when(kk < per_core)
        def _():
            assemble(kk)

        @pl.when(kk > 0)
        def _():
            propagate(kk - 1)

        return carry

    lax.fori_loop(0, per_core + 1, run, 0)

    def drain(kk, carry):
        for copy in out_copies(kk):
            copy.wait()
        for co, so in peers:
            block_copy(co, so, kk).wait_send()
        halo_copy(0, kk).wait_send()
        halo_copy(1, kk).wait_send()
        return carry

    lax.fori_loop(0, per_core, drain, 0)


def per_device(
    ncomp,
    nspace,
    spectrum,
    wind_speed,
    wind_dir,
    ocean_mask,
    turning,
    u_current,
    group_courant,
    growth_rate,
    dissipation,
    comp_owner,
):
    rows, strip, ncomps = spectrum.shape
    nfreqs = group_courant.shape[0]
    ndirs = ncomps // nfreqs
    nd = ndirs // ncomp
    owned = nfreqs // ncomp
    per_core = owned // 2
    npeer = ncomp * 2
    packs = ndirs // PER_PACK
    xt = jnp.transpose(spectrum, (2, 0, 1))
    maskf = ocean_mask.astype(jnp.float32)
    current = jnp.broadcast_to(u_current[:, None], (rows, LANES))
    angles = (2.0 * math.pi * np.arange(ndirs, dtype=np.float32) / ndirs).astype(np.float32)
    cosines = jnp.asarray(np.cos(angles.astype(np.float64)).astype(np.float32))
    sines = jnp.asarray(np.sin(angles.astype(np.float64)).astype(np.float32))
    vmem = pl.BlockSpec(memory_space=pltpu.VMEM)
    smem = pl.BlockSpec(memory_space=pltpu.SMEM)
    dma = pltpu.SemaphoreType.DMA
    tile = (ROWS, LANES)

    def scratch(*lead):
        return pltpu.VMEM(lead + tile, jnp.float32)

    return pl.pallas_call(
        functools.partial(kernel, (ncomp, nspace, ndirs, nfreqs, per_core)),
        out_shape=jax.ShapeDtypeStruct((owned, ndirs, rows, LANES), jnp.float32),
        in_specs=[vmem] * 6 + [smem] * 6,
        out_specs=pl.BlockSpec(memory_space=pl.ANY),
        scratch_shapes=[
            scratch(nd),
            pltpu.VMEM((4, ROWS, strip), jnp.float32),
            scratch(npeer, per_core, nd),
            scratch(npeer, per_core, nd),
            scratch(per_core, 2, ndirs),
            scratch(3),
            scratch(3),
            scratch(2),
            scratch(2),
            scratch(6),
            scratch(2, 5),
            scratch(2, per_core, 2 * packs),
            scratch(2, per_core, 2 * packs),
            scratch(2, 2, ndirs),
            scratch(per_core, 2, ndirs),
            dma((npeer, per_core)),
            dma((npeer, per_core)),
            dma((5,)),
            dma((5,)),
            dma((2, per_core)),
            dma((2, per_core)),
            dma((per_core,)),
            dma((per_core,)),
            dma((per_core,)),
        ],
        compiler_params=pltpu.CompilerParams(
            collective_id=0, has_side_effects=True, vmem_limit_bytes=40 * 1024 * 1024
        ),
        cost_estimate=pl.CostEstimate(flops=80_000_000, bytes_accessed=8_000_000, transcendentals=442368),
    )(
        xt,
        wind_speed,
        wind_dir,
        maskf,
        turning,
        current,
        group_courant,
        growth_rate,
        dissipation,
        comp_owner,
        cosines,
        sines,
    )


def solution(mesh):
    placed = (
        P(("groups", "sub"), ("space", "comp"), None),
        P(("groups", "sub"), ("space", "comp")),
        P(("groups", "sub"), ("space", "comp")),
        P("sub", "space"),
        P("sub", "space"),
        P("sub"),
        P(),
        P(),
        P(),
        P(),
    )
    return jax.shard_map(
        functools.partial(per_device, mesh.shape["comp"], mesh.shape["space"]),
        mesh=mesh,
        in_specs=placed,
        out_specs=P("comp", None, ("groups", "sub"), "space"),
        check_vma=False,
    )
```

```python
import functools
import math

import jax
import jax.numpy as jnp
import numpy as np
from jax import lax
from jax.experimental import pallas as pl
from jax.experimental.pallas import tpu as pltpu
from jax.sharding import PartitionSpec as P

NSUB = 4
HALO = 2 * NSUB
PER_PACK = 12
ROWS = 8
LANES = 128


def weights(courant):
    s = jnp.abs(courant)
    q = (1.0 - s * s) / 6.0
    sq = s * q
    up2 = -sq
    up1 = s * (0.5 + 0.5 * s) + 3.0 * sq
    mid = 1.0 - s * s - 3.0 * sq
    down = sq - s * (0.5 - 0.5 * s)
    return up2, up1, mid, down


def kernel(
    sizes,
    xt,
    wind_speed,
    wind_dir,
    mask,
    turning,
    current_hbm,
    speed_hbm,
    growth_hbm,
    loss_hbm,
    owner_hbm,
    out,
    current,
    speed,
    growth,
    loss,
    owner,
    param_sem,
    tables,
    level_part,
    sendbuf,
    recv,
    main,
    small,
    small_sib,
    small_left,
    small_right,
    mask_all,
    turn_all,
    halo_out,
    halo_in,
    lon_w,
    spin,
    res,
    send_sem,
    recv_sem,
    small_send,
    small_recv,
    halo_send,
    halo_recv,
    out_send,
    out_recv,
    own_sem,
):
    ncomp, nspace, ndirs, nfreqs, per_core = sizes
    strip = LANES // ncomp
    nd = ndirs // ncomp
    half = ndirs // 2
    packs = ndirs // PER_PACK
    me_c = lax.axis_index("comp")
    me_s = lax.axis_index("sub")
    me_z = lax.axis_index("space")
    other = 1 - me_s
    right = lax.rem(me_z + 1, nspace)
    left = lax.rem(me_z + nspace - 1, nspace)
    MESH = pl.DeviceIdType.MESH
    angles = (2.0 * math.pi * np.arange(ndirs, dtype=np.float32) / ndirs).astype(np.float64)
    cosines = [float(np.float32(np.cos(a))) for a in angles]
    sines = [float(np.float32(np.sin(a))) for a in angles]
    lane = lax.broadcasted_iota(jnp.int32, (ROWS, LANES), 1)
    row = lax.broadcasted_iota(jnp.int32, (ROWS, LANES), 0)

    def peer(co, so):
        return {"comp": lax.rem(me_c + co, ncomp), "sub": lax.rem(me_s + so, 2)}

    peers = [(co, so) for co in range(ncomp) for so in range(2) if co or so]
    near = [{"space": z, "sub": s} for z in (left, right) for s in (me_s, other)]
    barrier = pltpu.get_barrier_semaphore()
    for co, so in peers:
        pl.semaphore_signal(barrier, inc=1, device_id=peer(co, so), device_id_type=MESH)
    for to in near:
        pl.semaphore_signal(barrier, inc=1, device_id=to, device_id_type=MESH)

    params = [
        pltpu.make_async_copy(src, dst, param_sem.at[i])
        for i, (src, dst) in enumerate((
            (current_hbm, current),
            (speed_hbm, speed),
            (growth_hbm, growth),
            (loss_hbm, loss),
            (owner_hbm, owner),
        ))
    ]
    for copy in params:
        copy.start()
    level_part[...] = jnp.zeros_like(level_part)

    def add_level(f, carry):
        for part in range(4):
            block = xt[pl.ds(f * ndirs + part * (ndirs // 4), ndirs // 4)]
            level_part[part] += jnp.sum(block, axis=0)
        return carry

    lax.fori_loop(0, nfreqs, add_level, 0)
    level = (level_part[0] + level_part[1] + level_part[2] + level_part[3]) / (nfreqs * ndirs)
    level = level / (level + 0.25)

    def tiled(a):
        return jnp.concatenate([a] * ncomp, axis=1)

    level = tiled(level)
    wind = tiled(wind_speed[...])
    toward = tiled(wind_dir[...])
    group = (lane // strip) * nd
    for dd in range(nd):
        angle = 2.0 * math.pi * (group + dd).astype(jnp.float32) / ndirs
        tables[dd] = wind * jnp.maximum(jnp.cos(angle - toward), 0.0)

    for copy in params:
        copy.wait()
    flow = jnp.zeros((ROWS, LANES), jnp.float32)
    for j in range(ROWS):
        flow = jnp.where(row == j, current[j], flow)
    small[0] = mask[...].astype(jnp.float32)
    small[1] = turning[...]
    small[2] = flow
    pl.semaphore_wait(barrier, len(peers) + len(near))

    def fill(dst, at, co, so, kk):
        dest = peer(co, so)
        k = (dest["comp"] * 2 + dest["sub"]) * per_core + kk
        f = owner[k]
        g_rate = growth[f]
        d_rate = loss[f]
        for dd in range(nd):
            parts = [xt[f * ndirs + g * nd + dd] for g in range(ncomp)]
            tile = jnp.concatenate(parts, axis=1)
            dst[at, kk, dd] = tile * jnp.exp(g_rate * tables[dd] - d_rate * level)

    def block_copy(co, so, kk):
        r = co * 2 + so
        return pltpu.make_async_remote_copy(
            src_ref=sendbuf.at[r, kk],
            dst_ref=recv.at[r, kk],
            send_sem=send_sem.at[r, kk],
            recv_sem=recv_sem.at[r, kk],
            device_id=peer(co, so),
            device_id_type=MESH,
        )

    def send_far(kk, carry):
        for co, so in peers:
            if co:
                fill(sendbuf, co * 2 + so, co, so, kk)
                block_copy(co, so, kk).start()
        return carry

    lax.fori_loop(0, per_core, send_far, 0)

    def small_copies():
        sib = pltpu.make_async_remote_copy(
            src_ref=small, dst_ref=small_sib, send_sem=small_send.at[0], recv_sem=small_recv.at[0],
            device_id={"sub": other}, device_id_type=MESH)
        copies = [sib]
        for n, (z, land) in enumerate(((right, small_left), (left, small_right))):
            for so in range(2):
                i = 1 + 2 * n + so
                copies.append(pltpu.make_async_remote_copy(
                    src_ref=small.at[0], dst_ref=land.at[so], send_sem=small_send.at[i],
                    recv_sem=small_recv.at[i],
                    device_id={"space": z, "sub": lax.rem(me_s + so, 2)}, device_id_type=MESH))
        return copies

    for copy in small_copies():
        copy.start()

    def send_near(kk, carry):
        fill(sendbuf, 1, 0, 1, kk)
        block_copy(0, 1, kk).start()
        fill(recv, 0, 0, 0, kk)
        return carry

    lax.fori_loop(0, per_core, send_near, 0)

    for copy in small_copies():
        copy.wait()

    first = me_s == 0

    def both(own, sib):
        return jnp.where(first, own, sib), jnp.where(first, sib, own)

    def windows(lo, hi, lo_left, hi_left, lo_right, hi_right):
        acc = jnp.zeros((ROWS, LANES), jnp.float32)
        for base, own, l_halo, r_halo in ((0, lo, lo_left, lo_right), (64, hi, hi_left, hi_right)):
            for tile, start, count, at in (
                (own, LANES - 16, 16, 0),
                (r_halo, 0, HALO, 16),
                (l_halo, LANES - HALO, HALO, 24),
                (own, 0, 16, 32),
            ):
                moved = pltpu.roll(tile, (base + at - start) % LANES, 1)
                here = (lane >= base + at) & (lane < base + at + count)
                acc = jnp.where(here, moved, acc)
        return acc

    lo, hi = both(small[0], small_sib[0])
    lo_left, hi_left = both(small_left[0], small_left[1])
    lo_right, hi_right = both(small_right[0], small_right[1])
    mask_all[0] = lo
    mask_all[1] = hi
    mask_all[2] = windows(lo, hi, lo_left, hi_left, lo_right, hi_right)
    lo, hi = both(small[1], small_sib[1])
    for h, c in ((0, lo), (1, hi)):
        for i, w in enumerate(weights(c)):
            turn_all[h, i] = w
        turn_all[h, 4] = c
    lo, hi = both(small[2], small_sib[2])
    mask_all[3] = lo
    mask_all[4] = hi
    mask_all[5] = jnp.where(lane < 64, lo, hi)

    def halo_copy(side, kk):
        to = left if side == 0 else right
        return pltpu.make_async_remote_copy(
            src_ref=halo_out.at[side, kk],
            dst_ref=halo_in.at[side, kk],
            send_sem=halo_send.at[side, kk],
            recv_sem=halo_recv.at[side, kk],
            device_id={"space": to},
            device_id_type=MESH,
        )

    def assemble(kk):
        for co, so in peers:
            block_copy(co, so, kk).wait_recv()
        for h in range(2):
            so = lax.rem(h + me_s, 2)
            sea = mask_all[h]
            for dd in range(nd):
                got = [recv[lax.rem(me_c + ncomp - c, ncomp) * 2 + so, kk, dd] for c in range(ncomp)]
                for g in range(ncomp):
                    tile = got[0] if g == 0 else pltpu.roll(got[0], (LANES - g * strip) % LANES, 1)
                    for c in range(1, ncomp):
                        part = got[c]
                        if c != g:
                            part = pltpu.roll(part, ((c - g) * strip) % LANES, 1)
                        tile = jnp.where(lane < c * strip, tile, part)
                    main[kk, h, g * nd + dd] = tile * sea
            for q in range(packs):
                lows = highs = None
                for j in range(PER_PACK):
                    tile = main[kk, h, q * PER_PACK + j]
                    at = j * HALO
                    low = tile if at == 0 else pltpu.roll(tile, at, 1)
                    high = pltpu.roll(tile, at + HALO, 1)
                    lows = low if j == 0 else jnp.where(lane < at, lows, low)
                    highs = high if j == 0 else jnp.where(lane < at, highs, high)
                halo_out[0, kk, h * packs + q] = lows
                halo_out[1, kk, h * packs + q] = highs
        halo_copy(0, kk).start()
        halo_copy(1, kk).start()

    def along_lat(lo, hi, c, forward, sea_lo, sea_hi):
        up2, up1, mid, down = weights(c)
        for _ in range(NSUB):
            if forward:
                a, b = lo, hi

                def shift(n):
                    ra, rb = pltpu.roll(a, n, 0), pltpu.roll(b, n, 0)
                    return jnp.where(row < n, 0.0, ra), jnp.where(row < n, ra, rb)

                rb1, ra1 = pltpu.roll(hi, ROWS - 1, 0), pltpu.roll(lo, ROWS - 1, 0)
                lo_dn = jnp.where(row < ROWS - 1, ra1, rb1)
                hi_dn = jnp.where(row < ROWS - 1, rb1, 0.0)
            else:
                a, b = lo, hi

                def shift(n):
                    ra, rb = pltpu.roll(a, ROWS - n, 0), pltpu.roll(b, ROWS - n, 0)
                    return jnp.where(row < ROWS - n, ra, rb), jnp.where(row < ROWS - n, rb, 0.0)

                ra1, rb1 = pltpu.roll(lo, 1, 0), pltpu.roll(hi, 1, 0)
                lo_dn = jnp.where(row < 1, 0.0, ra1)
                hi_dn = jnp.where(row < 1, ra1, rb1)
            lo1, hi1 = shift(1)
            lo2, hi2 = shift(2)
            lo = (mid * lo + up1 * lo1 + (up2 * lo2 + down * lo_dn)) * sea_lo
            hi = (mid * hi + up1 * hi1 + (up2 * hi2 + down * hi_dn)) * sea_hi
        return lo, hi

    def propagate(kk):
        halo_copy(0, kk).wait_recv()
        halo_copy(1, kk).wait_recv()
        k = (me_c * 2 + me_s) * per_core + kk
        pace = speed[owner[k]]

        for q in range(packs):
            fields = []
            for j in range(PER_PACK):
                d = q * PER_PACK + j
                pieces = []
                for h in range(2):
                    tile = main[kk, h, d]
                    for source, start, at, end in (
                        (tile, LANES - 16, 0, 16),
                        (halo_in[0, kk, h * packs + q], j * HALO, 16, 24),
                        (halo_in[1, kk, h * packs + q], j * HALO, 24, 32),
                        (tile, 0, 32, 64),
                    ):
                        amount = (64 * h + at - start) % LANES
                        moved = source if amount == 0 else pltpu.roll(source, amount, 1)
                        pieces.append((64 * h + end, moved))
                edge = pieces[-1][1]
                for end, moved in reversed(pieces[:-1]):
                    edge = jnp.where(lane < end, moved, edge)
                c0 = pace * cosines[d]
                for i, tile in enumerate((main[kk, 0, d], main[kk, 1, d], edge)):
                    c = c0 + mask_all[3 + i]
                    up2, up1, mid, down = weights(c)
                    up = c > 0
                    lon_w[j * 3 + i, 0] = up2
                    lon_w[j * 3 + i, 1] = jnp.where(up, up1, down)
                    lon_w[j * 3 + i, 2] = mid
                    lon_w[j * 3 + i, 3] = jnp.where(up, down, up1)
                    lon_w[j * 3 + i, 4] = c
                    fields.append(tile)
            for step in range(NSUB):
                for n, f in enumerate(fields):
                    far = jnp.where(
                        lon_w[n, 4] > 0, pltpu.roll(f, 2, 1), pltpu.roll(f, LANES - 2, 1))
                    near_sum = lon_w[n, 1] * pltpu.roll(f, 1, 1) + lon_w[n, 3] * pltpu.roll(f, LANES - 1, 1)
                    f = (lon_w[n, 2] * f + lon_w[n, 0] * far + near_sum) * mask_all[n % 3]
                    fields[n] = f
            for j in range(PER_PACK):
                d = q * PER_PACK + j
                edge = fields[3 * j + 2]
                fixed = []
                for h in range(2):
                    base = 64 * h
                    tile = fields[3 * j + h]
                    head = pltpu.roll(edge, (LANES - base - 32) % LANES, 1)
                    tail = pltpu.roll(edge, (LANES - 16 - base) % LANES, 1)
                    tile = jnp.where(lane < HALO, head, tile)
                    fixed.append(jnp.where(lane < LANES - HALO, tile, tail))
                lo, hi = along_lat(
                    fixed[0], fixed[1], pace * sines[d], d < half, mask_all[0], mask_all[1])
                spin[0, 0, d] = lo
                spin[0, 1, d] = hi

        def turn(h, carry):
            up2, up1, mid, down = (turn_all[h, i] for i in range(4))
            up = turn_all[h, 4] > 0
            before, after = jnp.where(up, up1, down), jnp.where(up, down, up1)
            for step in range(NSUB):
                for d in range(ndirs):
                    f = [spin[step % 2, h, (d + n) % ndirs] for n in (-2, -1, 0, 1, 2)]
                    new = (mid * f[2] + up2 * jnp.where(up, f[0], f[4])) + (before * f[1] + after * f[3])
                    if step == NSUB - 1:
                        res[kk, h, d] = new
                    else:
                        spin[(step + 1) % 2, h, d] = new
            return carry

        lax.fori_loop(0, 2, turn, 0)
        for copy in out_copies(kk):
            copy.start()

    def out_copies(kk):
        slot = me_s * per_core + kk
        own = pltpu.make_async_copy(res.at[kk, me_s], out.at[slot], own_sem.at[kk])
        far = pltpu.make_async_remote_copy(
            src_ref=res.at[kk, other], dst_ref=out.at[slot], send_sem=out_send.at[kk],
            recv_sem=out_recv.at[kk], device_id={"sub": other}, device_id_type=MESH)
        return own, far

    def run(kk, carry):
        @pl.when(kk < per_core)
        def _():
            assemble(kk)

        @pl.when(kk > 0)
        def _():
            propagate(kk - 1)

        return carry

    lax.fori_loop(0, per_core + 1, run, 0)

    def drain(kk, carry):
        for copy in out_copies(kk):
            copy.wait()
        for co, so in peers:
            block_copy(co, so, kk).wait_send()
        halo_copy(0, kk).wait_send()
        halo_copy(1, kk).wait_send()
        return carry

    lax.fori_loop(0, per_core, drain, 0)


def per_device(
    ncomp,
    nspace,
    spectrum,
    wind_speed,
    wind_dir,
    ocean_mask,
    turning,
    u_current,
    group_courant,
    growth_rate,
    dissipation,
    comp_owner,
):
    rows, strip, ncomps = spectrum.shape
    nfreqs = group_courant.shape[0]
    ndirs = ncomps // nfreqs
    nd = ndirs // ncomp
    owned = nfreqs // ncomp
    per_core = owned // 2
    npeer = ncomp * 2
    packs = ndirs // PER_PACK
    xt = jnp.transpose(spectrum, (2, 0, 1))
    vmem = pl.BlockSpec(memory_space=pltpu.VMEM)
    dma = pltpu.SemaphoreType.DMA
    tile = (ROWS, LANES)

    def scratch(*lead):
        return pltpu.VMEM(lead + tile, jnp.float32)

    return pl.pallas_call(
        functools.partial(kernel, (ncomp, nspace, ndirs, nfreqs, per_core)),
        out_shape=jax.ShapeDtypeStruct((owned, ndirs, rows, LANES), jnp.float32),
        in_specs=[vmem] * 5 + [pl.BlockSpec(memory_space=pl.ANY)] * 5,
        out_specs=pl.BlockSpec(memory_space=pl.ANY),
        scratch_shapes=[
            pltpu.SMEM((rows,), jnp.float32),
            pltpu.SMEM((nfreqs,), jnp.float32),
            pltpu.SMEM((nfreqs,), jnp.float32),
            pltpu.SMEM((nfreqs,), jnp.float32),
            pltpu.SMEM((nfreqs,), jnp.int32),
            dma((5,)),
            scratch(nd),
            pltpu.VMEM((4, ROWS, strip), jnp.float32),
            scratch(npeer, per_core, nd),
            scratch(npeer, per_core, nd),
            scratch(per_core, 2, ndirs),
            scratch(3),
            scratch(3),
            scratch(2),
            scratch(2),
            scratch(6),
            scratch(2, 5),
            scratch(2, per_core, 2 * packs),
            scratch(2, per_core, 2 * packs),
            scratch(3 * PER_PACK, 5),
            scratch(2, 2, ndirs),
            scratch(per_core, 2, ndirs),
            dma((npeer, per_core)),
            dma((npeer, per_core)),
            dma((5,)),
            dma((5,)),
            dma((2, per_core)),
            dma((2, per_core)),
            dma((per_core,)),
            dma((per_core,)),
            dma((per_core,)),
        ],
        compiler_params=pltpu.CompilerParams(
            collective_id=0, has_side_effects=True, vmem_limit_bytes=40 * 1024 * 1024
        ),
        cost_estimate=pl.CostEstimate(flops=80_000_000, bytes_accessed=8_000_000, transcendentals=442368),
    )(
        xt,
        wind_speed,
        wind_dir,
        ocean_mask,
        turning,
        u_current,
        group_courant,
        growth_rate,
        dissipation,
        comp_owner,
    )


def solution(mesh):
    placed = (
        P(("groups", "sub"), ("space", "comp"), None),
        P(("groups", "sub"), ("space", "comp")),
        P(("groups", "sub"), ("space", "comp")),
        P("sub", "space"),
        P("sub", "space"),
        P("sub"),
        P(),
        P(),
        P(),
        P(),
    )
    return jax.shard_map(
        functools.partial(per_device, mesh.shape["comp"], mesh.shape["space"]),
        mesh=mesh,
        in_specs=placed,
        out_specs=P("comp", None, ("groups", "sub"), "space"),
        check_vma=False,
    )
```

```python
import functools
import math

import jax
import jax.numpy as jnp
import numpy as np
from jax import lax
from jax.experimental import pallas as pl
from jax.experimental.pallas import tpu as pltpu
from jax.sharding import PartitionSpec as P

NSUB = 4
HALO = 2 * NSUB
PER_PACK = 12
ROWS = 8
LANES = 128


def weights(courant):
    s = jnp.abs(courant)
    q = (1.0 - s * s) / 6.0
    sq = s * q
    up2 = -sq
    up1 = s * (0.5 + 0.5 * s) + 3.0 * sq
    mid = 1.0 - s * s - 3.0 * sq
    down = sq - s * (0.5 - 0.5 * s)
    return up2, up1, mid, down


def kernel(
    sizes,
    xt,
    wind_speed,
    wind_dir,
    mask,
    turning,
    rates_hbm,
    owner_hbm,
    out,
    rates,
    owner,
    param_sem,
    tables,
    level_part,
    sendbuf,
    recv,
    main,
    small,
    small_sib,
    small_left,
    small_right,
    mask_all,
    turn_all,
    halo_out,
    halo_in,
    lon_w,
    spin,
    res,
    send_sem,
    recv_sem,
    small_send,
    small_recv,
    halo_send,
    halo_recv,
    out_send,
    out_recv,
    own_sem,
):
    ncomp, nspace, ndirs, nfreqs, per_core = sizes
    strip = LANES // ncomp
    nd = ndirs // ncomp
    half = ndirs // 2
    packs = ndirs // PER_PACK
    me_c = lax.axis_index("comp")
    me_s = lax.axis_index("sub")
    me_z = lax.axis_index("space")
    other = 1 - me_s
    right = lax.rem(me_z + 1, nspace)
    left = lax.rem(me_z + nspace - 1, nspace)
    MESH = pl.DeviceIdType.MESH
    angles = (2.0 * math.pi * np.arange(ndirs, dtype=np.float32) / ndirs).astype(np.float64)
    cosines = [float(np.float32(np.cos(a))) for a in angles]
    sines = [float(np.float32(np.sin(a))) for a in angles]
    lane = lax.broadcasted_iota(jnp.int32, (ROWS, LANES), 1)
    row = lax.broadcasted_iota(jnp.int32, (ROWS, LANES), 0)

    def peer(co, so):
        return {"comp": lax.rem(me_c + co, ncomp), "sub": lax.rem(me_s + so, 2)}

    peers = [(co, so) for co in range(ncomp) for so in range(2) if co or so]
    near = [{"space": z, "sub": s} for z in (left, right) for s in (me_s, other)]
    barrier = pltpu.get_barrier_semaphore()
    for co, so in peers:
        pl.semaphore_signal(barrier, inc=1, device_id=peer(co, so), device_id_type=MESH)
    for to in near:
        pl.semaphore_signal(barrier, inc=1, device_id=to, device_id_type=MESH)

    params = [
        pltpu.make_async_copy(src, dst, param_sem.at[i])
        for i, (src, dst) in enumerate((
            (rates_hbm, rates),
            (owner_hbm, owner),
        ))
    ]
    for copy in params:
        copy.start()
    level_part[...] = jnp.zeros_like(level_part)

    def add_level(f, carry):
        for part in range(4):
            block = xt[pl.ds(f * ndirs + part * (ndirs // 4), ndirs // 4)]
            level_part[part] += jnp.sum(block, axis=0)
        return carry

    lax.fori_loop(0, nfreqs, add_level, 0)
    level = (level_part[0] + level_part[1] + level_part[2] + level_part[3]) / (nfreqs * ndirs)
    level = level / (level + 0.25)

    def tiled(a):
        return jnp.concatenate([a] * ncomp, axis=1)

    level = tiled(level)
    wind = tiled(wind_speed[...])
    toward = tiled(wind_dir[...])
    group = (lane // strip) * nd
    for dd in range(nd):
        angle = 2.0 * math.pi * (group + dd).astype(jnp.float32) / ndirs
        tables[dd] = wind * jnp.maximum(jnp.cos(angle - toward), 0.0)

    for copy in params:
        copy.wait()
    flow = jnp.zeros((ROWS, LANES), jnp.float32)
    for j in range(ROWS):
        flow = jnp.where(row == j, rates[3 * nfreqs + j], flow)
    small[0] = mask[...].astype(jnp.float32)
    small[1] = turning[...]
    small[2] = flow
    pl.semaphore_wait(barrier, len(peers) + len(near))

    def fill(dst, at, co, so, kk):
        dest = peer(co, so)
        k = (dest["comp"] * 2 + dest["sub"]) * per_core + kk
        f = owner[k]
        g_rate = rates[nfreqs + f]
        d_rate = rates[2 * nfreqs + f]
        for dd in range(nd):
            parts = [xt[f * ndirs + g * nd + dd] for g in range(ncomp)]
            tile = jnp.concatenate(parts, axis=1)
            dst[at, kk, dd] = tile * jnp.exp(g_rate * tables[dd] - d_rate * level)

    def block_copy(co, so, kk):
        r = co * 2 + so
        return pltpu.make_async_remote_copy(
            src_ref=sendbuf.at[r, kk],
            dst_ref=recv.at[r, kk],
            send_sem=send_sem.at[r, kk],
            recv_sem=recv_sem.at[r, kk],
            device_id=peer(co, so),
            device_id_type=MESH,
        )

    def send_far(kk, carry):
        for co, so in peers:
            if co:
                fill(sendbuf, co * 2 + so, co, so, kk)
                block_copy(co, so, kk).start()
        return carry

    lax.fori_loop(0, per_core, send_far, 0)

    def small_copies():
        sib = pltpu.make_async_remote_copy(
            src_ref=small, dst_ref=small_sib, send_sem=small_send.at[0], recv_sem=small_recv.at[0],
            device_id={"sub": other}, device_id_type=MESH)
        copies = [sib]
        for n, (z, land) in enumerate(((right, small_left), (left, small_right))):
            for so in range(2):
                i = 1 + 2 * n + so
                copies.append(pltpu.make_async_remote_copy(
                    src_ref=small.at[0], dst_ref=land.at[so], send_sem=small_send.at[i],
                    recv_sem=small_recv.at[i],
                    device_id={"space": z, "sub": lax.rem(me_s + so, 2)}, device_id_type=MESH))
        return copies

    for copy in small_copies():
        copy.start()

    def send_near(kk, carry):
        fill(sendbuf, 1, 0, 1, kk)
        block_copy(0, 1, kk).start()
        fill(recv, 0, 0, 0, kk)
        return carry

    lax.fori_loop(0, per_core, send_near, 0)

    for copy in small_copies():
        copy.wait()

    first = me_s == 0

    def both(own, sib):
        return jnp.where(first, own, sib), jnp.where(first, sib, own)

    def windows(lo, hi, lo_left, hi_left, lo_right, hi_right):
        acc = jnp.zeros((ROWS, LANES), jnp.float32)
        for base, own, l_halo, r_halo in ((0, lo, lo_left, lo_right), (64, hi, hi_left, hi_right)):
            for tile, start, count, at in (
                (own, LANES - 16, 16, 0),
                (r_halo, 0, HALO, 16),
                (l_halo, LANES - HALO, HALO, 24),
                (own, 0, 16, 32),
            ):
                moved = pltpu.roll(tile, (base + at - start) % LANES, 1)
                here = (lane >= base + at) & (lane < base + at + count)
                acc = jnp.where(here, moved, acc)
        return acc

    lo, hi = both(small[0], small_sib[0])
    lo_left, hi_left = both(small_left[0], small_left[1])
    lo_right, hi_right = both(small_right[0], small_right[1])
    mask_all[0] = lo
    mask_all[1] = hi
    mask_all[2] = windows(lo, hi, lo_left, hi_left, lo_right, hi_right)
    lo, hi = both(small[1], small_sib[1])
    for h, c in ((0, lo), (1, hi)):
        for i, w in enumerate(weights(c)):
            turn_all[h, i] = w
        turn_all[h, 4] = c
    lo, hi = both(small[2], small_sib[2])
    mask_all[3] = lo
    mask_all[4] = hi
    mask_all[5] = jnp.where(lane < 64, lo, hi)

    def halo_copy(side, kk):
        to = left if side == 0 else right
        return pltpu.make_async_remote_copy(
            src_ref=halo_out.at[side, kk],
            dst_ref=halo_in.at[side, kk],
            send_sem=halo_send.at[side, kk],
            recv_sem=halo_recv.at[side, kk],
            device_id={"space": to},
            device_id_type=MESH,
        )

    def assemble(kk):
        for co, so in peers:
            block_copy(co, so, kk).wait_recv()
        for h in range(2):
            so = lax.rem(h + me_s, 2)
            sea = mask_all[h]
            for dd in range(nd):
                got = [recv[lax.rem(me_c + ncomp - c, ncomp) * 2 + so, kk, dd] for c in range(ncomp)]
                for g in range(ncomp):
                    tile = got[0] if g == 0 else pltpu.roll(got[0], (LANES - g * strip) % LANES, 1)
                    for c in range(1, ncomp):
                        part = got[c]
                        if c != g:
                            part = pltpu.roll(part, ((c - g) * strip) % LANES, 1)
                        tile = jnp.where(lane < c * strip, tile, part)
                    main[kk, h, g * nd + dd] = tile * sea
            for q in range(packs):
                lows = highs = None
                for j in range(PER_PACK):
                    tile = main[kk, h, q * PER_PACK + j]
                    at = j * HALO
                    low = tile if at == 0 else pltpu.roll(tile, at, 1)
                    high = pltpu.roll(tile, at + HALO, 1)
                    lows = low if j == 0 else jnp.where(lane < at, lows, low)
                    highs = high if j == 0 else jnp.where(lane < at, highs, high)
                halo_out[0, kk, h * packs + q] = lows
                halo_out[1, kk, h * packs + q] = highs
        halo_copy(0, kk).start()
        halo_copy(1, kk).start()

    def along_lat(lo, hi, c, forward, sea_lo, sea_hi):
        up2, up1, mid, down = weights(c)
        for _ in range(NSUB):
            if forward:
                a, b = lo, hi

                def shift(n):
                    ra, rb = pltpu.roll(a, n, 0), pltpu.roll(b, n, 0)
                    return jnp.where(row < n, 0.0, ra), jnp.where(row < n, ra, rb)

                rb1, ra1 = pltpu.roll(hi, ROWS - 1, 0), pltpu.roll(lo, ROWS - 1, 0)
                lo_dn = jnp.where(row < ROWS - 1, ra1, rb1)
                hi_dn = jnp.where(row < ROWS - 1, rb1, 0.0)
            else:
                a, b = lo, hi

                def shift(n):
                    ra, rb = pltpu.roll(a, ROWS - n, 0), pltpu.roll(b, ROWS - n, 0)
                    return jnp.where(row < ROWS - n, ra, rb), jnp.where(row < ROWS - n, rb, 0.0)

                ra1, rb1 = pltpu.roll(lo, 1, 0), pltpu.roll(hi, 1, 0)
                lo_dn = jnp.where(row < 1, 0.0, ra1)
                hi_dn = jnp.where(row < 1, ra1, rb1)
            lo1, hi1 = shift(1)
            lo2, hi2 = shift(2)
            lo = (mid * lo + up1 * lo1 + (up2 * lo2 + down * lo_dn)) * sea_lo
            hi = (mid * hi + up1 * hi1 + (up2 * hi2 + down * hi_dn)) * sea_hi
        return lo, hi

    def propagate(kk):
        halo_copy(0, kk).wait_recv()
        halo_copy(1, kk).wait_recv()
        k = (me_c * 2 + me_s) * per_core + kk
        pace = rates[owner[k]]

        for q in range(packs):
            fields = []
            for j in range(PER_PACK):
                d = q * PER_PACK + j
                pieces = []
                for h in range(2):
                    tile = main[kk, h, d]
                    for source, start, at, end in (
                        (tile, LANES - 16, 0, 16),
                        (halo_in[0, kk, h * packs + q], j * HALO, 16, 24),
                        (halo_in[1, kk, h * packs + q], j * HALO, 24, 32),
                        (tile, 0, 32, 64),
                    ):
                        amount = (64 * h + at - start) % LANES
                        moved = source if amount == 0 else pltpu.roll(source, amount, 1)
                        pieces.append((64 * h + end, moved))
                edge = pieces[-1][1]
                for end, moved in reversed(pieces[:-1]):
                    edge = jnp.where(lane < end, moved, edge)
                c0 = pace * cosines[d]
                for i, tile in enumerate((main[kk, 0, d], main[kk, 1, d], edge)):
                    c = c0 + mask_all[3 + i]
                    up2, up1, mid, down = weights(c)
                    up = c > 0
                    lon_w[j * 3 + i, 0] = up2
                    lon_w[j * 3 + i, 1] = jnp.where(up, up1, down)
                    lon_w[j * 3 + i, 2] = mid
                    lon_w[j * 3 + i, 3] = jnp.where(up, down, up1)
                    lon_w[j * 3 + i, 4] = c
                    fields.append(tile)
            for step in range(NSUB):
                for n, f in enumerate(fields):
                    far = jnp.where(
                        lon_w[n, 4] > 0, pltpu.roll(f, 2, 1), pltpu.roll(f, LANES - 2, 1))
                    near_sum = lon_w[n, 1] * pltpu.roll(f, 1, 1) + lon_w[n, 3] * pltpu.roll(f, LANES - 1, 1)
                    f = (lon_w[n, 2] * f + lon_w[n, 0] * far + near_sum) * mask_all[n % 3]
                    fields[n] = f
            for j in range(PER_PACK):
                d = q * PER_PACK + j
                edge = fields[3 * j + 2]
                fixed = []
                for h in range(2):
                    base = 64 * h
                    tile = fields[3 * j + h]
                    head = pltpu.roll(edge, (LANES - base - 32) % LANES, 1)
                    tail = pltpu.roll(edge, (LANES - 16 - base) % LANES, 1)
                    tile = jnp.where(lane < HALO, head, tile)
                    fixed.append(jnp.where(lane < LANES - HALO, tile, tail))
                lo, hi = along_lat(
                    fixed[0], fixed[1], pace * sines[d], d < half, mask_all[0], mask_all[1])
                spin[0, 0, d] = lo
                spin[0, 1, d] = hi

        def turn(h, carry):
            up2, up1, mid, down = (turn_all[h, i] for i in range(4))
            up = turn_all[h, 4] > 0
            before, after = jnp.where(up, up1, down), jnp.where(up, down, up1)
            for step in range(NSUB):
                for d in range(ndirs):
                    f = [spin[step % 2, h, (d + n) % ndirs] for n in (-2, -1, 0, 1, 2)]
                    new = (mid * f[2] + up2 * jnp.where(up, f[0], f[4])) + (before * f[1] + after * f[3])
                    if step == NSUB - 1:
                        res[kk, h, d] = new
                    else:
                        spin[(step + 1) % 2, h, d] = new
            return carry

        lax.fori_loop(0, 2, turn, 0)
        for copy in out_copies(kk):
            copy.start()

    def out_copies(kk):
        slot = me_s * per_core + kk
        own = pltpu.make_async_copy(res.at[kk, me_s], out.at[slot], own_sem.at[kk])
        far = pltpu.make_async_remote_copy(
            src_ref=res.at[kk, other], dst_ref=out.at[slot], send_sem=out_send.at[kk],
            recv_sem=out_recv.at[kk], device_id={"sub": other}, device_id_type=MESH)
        return own, far

    def run(kk, carry):
        @pl.when(kk < per_core)
        def _():
            assemble(kk)

        @pl.when(kk > 0)
        def _():
            propagate(kk - 1)

        return carry

    lax.fori_loop(0, per_core + 1, run, 0)

    def drain(kk, carry):
        for copy in out_copies(kk):
            copy.wait()
        for co, so in peers:
            block_copy(co, so, kk).wait_send()
        halo_copy(0, kk).wait_send()
        halo_copy(1, kk).wait_send()
        return carry

    lax.fori_loop(0, per_core, drain, 0)


def per_device(
    ncomp,
    nspace,
    spectrum,
    wind_speed,
    wind_dir,
    ocean_mask,
    turning,
    u_current,
    group_courant,
    growth_rate,
    dissipation,
    comp_owner,
):
    rows, strip, ncomps = spectrum.shape
    nfreqs = group_courant.shape[0]
    ndirs = ncomps // nfreqs
    nd = ndirs // ncomp
    owned = nfreqs // ncomp
    per_core = owned // 2
    npeer = ncomp * 2
    packs = ndirs // PER_PACK
    xt = jnp.transpose(spectrum, (2, 0, 1))
    rates = jnp.concatenate([group_courant, growth_rate, dissipation, u_current])
    vmem = pl.BlockSpec(memory_space=pltpu.VMEM)
    dma = pltpu.SemaphoreType.DMA
    tile = (ROWS, LANES)

    def scratch(*lead):
        return pltpu.VMEM(lead + tile, jnp.float32)

    return pl.pallas_call(
        functools.partial(kernel, (ncomp, nspace, ndirs, nfreqs, per_core)),
        out_shape=jax.ShapeDtypeStruct((owned, ndirs, rows, LANES), jnp.float32),
        in_specs=[vmem] * 5 + [pl.BlockSpec(memory_space=pl.ANY)] * 2,
        out_specs=pl.BlockSpec(memory_space=pl.ANY),
        scratch_shapes=[
            pltpu.SMEM((3 * nfreqs + rows,), jnp.float32),
            pltpu.SMEM((nfreqs,), jnp.int32),
            dma((2,)),
            scratch(nd),
            pltpu.VMEM((4, ROWS, strip), jnp.float32),
            scratch(npeer, per_core, nd),
            scratch(npeer, per_core, nd),
            scratch(per_core, 2, ndirs),
            scratch(3),
            scratch(3),
            scratch(2),
            scratch(2),
            scratch(6),
            scratch(2, 5),
            scratch(2, per_core, 2 * packs),
            scratch(2, per_core, 2 * packs),
            scratch(3 * PER_PACK, 5),
            scratch(2, 2, ndirs),
            scratch(per_core, 2, ndirs),
            dma((npeer, per_core)),
            dma((npeer, per_core)),
            dma((5,)),
            dma((5,)),
            dma((2, per_core)),
            dma((2, per_core)),
            dma((per_core,)),
            dma((per_core,)),
            dma((per_core,)),
        ],
        compiler_params=pltpu.CompilerParams(
            collective_id=0, has_side_effects=True, vmem_limit_bytes=40 * 1024 * 1024
        ),
        cost_estimate=pl.CostEstimate(flops=80_000_000, bytes_accessed=8_000_000, transcendentals=442368),
    )(
        xt,
        wind_speed,
        wind_dir,
        ocean_mask,
        turning,
        rates,
        comp_owner,
    )


def solution(mesh):
    placed = (
        P(("groups", "sub"), ("space", "comp"), None),
        P(("groups", "sub"), ("space", "comp")),
        P(("groups", "sub"), ("space", "comp")),
        P("sub", "space"),
        P("sub", "space"),
        P("sub"),
        P(),
        P(),
        P(),
        P(),
    )
    return jax.shard_map(
        functools.partial(per_device, mesh.shape["comp"], mesh.shape["space"]),
        mesh=mesh,
        in_specs=placed,
        out_specs=P("comp", None, ("groups", "sub"), "space"),
        check_vma=False,
    )
```
